256 devices in a mesh: vid: 8 (over z_hi, x), ta: 4 (over z_lo), ha: 8 (over y, core).
Axes of the slice: x: 4, y: 4, z: 8 (z_hi: 2, z_lo: 4; z = z_hi * 4 + z_lo), core: 2. Of those that a mesh axis runs over, the one named last changes fastest.
Arguments:
- queries: bfloat16 [128, 64, 16, 1536], P(('vid', 'ta'), 'ha'), parts along dimension 0, may hold values from -4.5 to 4.5
- keys: bfloat16 [128, 64, 16, 1536], P(('vid', 'ta'), 'ha'), parts along dimension 0, may hold values from -4.5 to 4.5
- values: bfloat16 [128, 64, 16, 1536], P(('vid', 'ta'), 'ha'), parts along dimension 0, may hold values from -6 to 6
- far_tiles: int32 [512, 12, 4], P(('vid', 'ta', 'ha')), parts along dimension 0, may hold values from 0 to 63, as said below
Outputs:
- attended: bfloat16 [128, 64, 16, 1536], P(('vid', 'ta'), 'ha'), parts along dimension 0
The draws below stay inside these ranges and needn't reach their ends.
There are 8 independent parts, one for each index of `vid`. The reference program is written for one: setup_inputs(seed, part) draws one part's arguments, and reference() takes and returns one part's arrays. A program takes and returns all parts, laid end to end along the dimension named above; each array names one. Nothing has to cross between parts.
Inputs may be any that keep to these rules, and one draw needn't show every extreme that they name: `far_tiles`: every id names a tile of the same video. Among the 2 x 12 x 4 entries of one slab's query tiles, at most 4 name tiles of any one slab, and exactly 4 name tiles of some slab.
All inputs are finite; a program needn't handle non-finite values.
Results may differ from the reference program's by a relative error of at most 0.0059.
Values may be sent and summed in bfloat16 or wider, within the bound.
A program may use at most 192 MiB of HBM per device.

```python
import jax
import jax.numpy as jnp
from jax import lax

HEADS = 12
HD = 128
FAR = 4
TILE_F = 4
TILE_H = 8
TILE_W = 8
WIDTH = 16
WT = 2
FRAMES = 16
HEIGHT = 64
OWNERS = 32
TILES = 64
CAP = 4


def draw_queries(key, part):
    key = jax.random.fold_in(key, 1)
    shape = (FRAMES, HEIGHT, WIDTH, HEADS * HD)
    return jnp.clip(jax.random.normal(key, shape), -4.5, 4.5).astype(jnp.bfloat16)


def draw_keys(key, part):
    key = jax.random.fold_in(key, 2)
    shape = (FRAMES, HEIGHT, WIDTH, HEADS * HD)
    return jnp.clip(jax.random.normal(key, shape), -4.5, 4.5).astype(jnp.bfloat16)


def draw_far_tiles(key, part):
    key = jax.random.fold_in(key, 3)
    count = WT * HEADS * FAR
    slots = OWNERS * CAP

    def one_slab(slab):
        sub = jax.random.fold_in(key, slab)
        chosen = jax.random.randint(jax.random.fold_in(sub, 1), (), 0, OWNERS)
        shuffled = jax.random.permutation(jax.random.fold_in(sub, 2), jnp.arange(slots, dtype=jnp.int32))
        order_key = jnp.where(shuffled // CAP == chosen, 0, slots) + jnp.arange(slots, dtype=jnp.int32)
        picked = shuffled[jnp.argsort(order_key)][:count]
        picked = jax.random.permutation(jax.random.fold_in(sub, 3), picked)
        local = jax.random.randint(jax.random.fold_in(sub, 4), (count,), 0, WT)
        return (picked // CAP * WT + local).astype(jnp.int32)
    lists = jax.vmap(one_slab)(jnp.arange(OWNERS, dtype=jnp.int32))
    return lists.reshape(TILES, HEADS, FAR)


def block_levels(own_key, shape, shards, least, largest):
    factor_of, own = 1.0, jax.random.fold_in(own_key, 6)
    for axis_at, blocks in shards:
        steps = jnp.exp(jax.random.uniform(jax.random.fold_in(own, axis_at), (blocks,), jnp.float32, least / len(shards), largest / len(shards)))
        factor_of = factor_of * jnp.repeat(steps, shape[axis_at] // blocks).reshape([-1 if axis == axis_at else 1 for axis in range(len(shape))])
    return factor_of


def scatter_about(rng, shape, spread, limit, pieces=(), held_as=jnp.bfloat16):
    values = jax.random.normal(rng, shape, jnp.float32) * spread
    if len(pieces) > 0:
        values = block_levels(rng, shape, pieces, -0.22, 0.18) * values
    return jnp.clip(values, min=-limit, max=limit).astype(held_as)


def setup_inputs(seed: int = 0, part: int = 0) -> dict:
    arg_keys = jax.random.split(jax.random.key(seed), 5)
    part_keys = jax.random.split(jax.random.fold_in(arg_keys[4], part), 5)
    queries = draw_queries(jax.random.fold_in(jax.random.fold_in(arg_keys[4], part), 71), part)
    keys = draw_keys(jax.random.fold_in(jax.random.fold_in(arg_keys[4], part), 71), part)
    values = scatter_about(part_keys[2], (FRAMES, HEIGHT, WIDTH, HEADS * HD), 1.0, 6.0, ((0, 4), (1, 8)))
    far_tiles = draw_far_tiles(jax.random.fold_in(jax.random.fold_in(arg_keys[4], part), 71), part)
    return dict(queries=queries, keys=keys, values=values, far_tiles=far_tiles)


def tiles_of(block):
    frames, rows, cols, chans = block.shape
    shaped = block.reshape(frames // TILE_F, TILE_F, rows // TILE_H, TILE_H, cols // TILE_W, TILE_W, HEADS, HD)
    shaped = jnp.transpose(shaped, (0, 2, 4, 6, 1, 3, 5, 7))
    return shaped.reshape(-1, HEADS, TILE_F * TILE_H * TILE_W, HD)


def reference(queries, keys, values, far_tiles):
    count_t = FRAMES // TILE_F
    count_h = HEIGHT // TILE_H
    count_w = WIDTH // TILE_W
    q_tiles = tiles_of(queries)
    k_tiles = tiles_of(keys)
    v_tiles = tiles_of(values)
    scale = HD ** -0.5
    offsets = [(0, 0), (-1, 0), (1, 0), (0, -1), (0, 1)]
    head_ids = jnp.arange(HEADS, dtype=jnp.int32)[:, None]

    def one_tile(index):
        t_pos = index // (count_h * count_w)
        h_pos = (index // count_w) % count_h
        w_pos = index % count_w
        ids = []
        valid = []
        for step_t, step_h in offsets:
            for step_w in (-1, 0, 1):
                tt = t_pos + step_t
                hh = h_pos + step_h
                ww = w_pos + step_w
                inside = (tt >= 0) & (tt < count_t) & (hh >= 0) & (hh < count_h) & (ww >= 0) & (ww < count_w)
                ids.append(jnp.where(inside, (tt * count_h + hh) * count_w + ww, 0).astype(jnp.int32))
                valid.append(inside)
        ids = jnp.stack(ids)
        valid = jnp.stack(valid)
        q_tile = q_tiles[index].astype(jnp.float32)
        k_near = k_tiles[ids].astype(jnp.float32)
        v_near = v_tiles[ids].astype(jnp.float32)
        near = jnp.einsum("nqd,cnkd->nqck", q_tile, k_near) * scale
        near = jnp.where(valid[None, None, :, None], near, -1e30)
        far_ids = far_tiles[index].astype(jnp.int32)
        k_far = k_tiles[far_ids, head_ids].astype(jnp.float32)
        v_far = v_tiles[far_ids, head_ids].astype(jnp.float32)
        distant = jnp.einsum("nqd,nfkd->nqfk", q_tile, k_far) * scale
        top = jnp.maximum(jnp.max(near, axis=(2, 3)), jnp.max(distant, axis=(2, 3)))
        p_near = jnp.exp(near - top[:, :, None, None]).astype(jnp.bfloat16).astype(jnp.float32)
        p_far = jnp.exp(distant - top[:, :, None, None]).astype(jnp.bfloat16).astype(jnp.float32)
        total = jnp.sum(p_near, axis=(2, 3)) + jnp.sum(p_far, axis=(2, 3))
        accum = jnp.einsum("nqck,cnkd->nqd", p_near, v_near) + jnp.einsum("nqfk,nfkd->nqd", p_far, v_far)
        return (accum / total[:, :, None]).astype(jnp.bfloat16)

    result = lax.map(one_tile, jnp.arange(TILES, dtype=jnp.int32))
    result = result.reshape(count_t, count_h, count_w, HEADS, TILE_F, TILE_H, TILE_W, HD)
    result = jnp.transpose(result, (0, 4, 1, 5, 2, 6, 3, 7))
    return result.reshape(FRAMES, HEIGHT, WIDTH, HEADS * HD)
```

```python
import functools

import jax
import jax.numpy as jnp
from jax import lax
from jax.experimental import pallas as pl
from jax.experimental.pallas import tpu as pltpu
from jax.sharding import PartitionSpec as P

HEADS = 12
HD = 128
FAR = 4
NT = 4
NH = 8
NY = 4
GROUP = HEADS // NT
TILE = 256
SLAB = 512
KEYS = 5 * SLAB + FAR * TILE
EXP2_SCALE = HD**-0.5 * 1.4426950408889634
MASKED = -1e30
MESH = pl.DeviceIdType.MESH

STEPS = (
    ("C", 0, 1), ("D", 0, 0), ("C", 0, 2), ("D", 0, 1), ("C", 1, 1), ("C", 0, 3), ("D", 0, 2), ("E", 0, 0),
    ("D", 1, 0), ("C", 1, 2), ("D", 0, 3), ("E", 0, 1), ("D", 1, 1), ("C", 2, 1), ("C", 1, 3), ("E", 0, 2),
    ("D", 1, 2), ("D", 2, 0), ("C", 2, 2), ("E", 0, 3), ("E", 1, 0), ("C", 2, 3), ("Q", 0, 0), ("E", 1, 1),
    ("D", 1, 3), ("X", 0, 0), ("D", 2, 1), ("E", 1, 2), ("D", 2, 2), ("E", 1, 3), ("X", 1, 0),
    ("D", 2, 3), ("E", 2, 0), ("E", 2, 1), ("E", 2, 2), ("E", 2, 3), ("X", 2, 0), ("W", 0, 0), ("W", 1, 0), ("W", 2, 0),
)


def untile(block):
    x = block.astype(jnp.float32).reshape(32, 2, 8, HD)
    return [x[:, w].reshape(TILE, HD).astype(jnp.bfloat16) for w in range(2)]


def kernel(
    q_hbm, k_hbm, v_hbm, far_in, out_hbm,
    out, q_in, k_in, v_in, kv_out, q_out, t0, t1, t2, q_all, o_out, o_in, far_all, scores,
    load_sem, own_sem, out_sem, far_s, far_r, z_s, z_r, q_s, q_r, o_s, o_r, y_s, y_r,
):
    tables = (t0, t1, t2)
    z = lax.axis_index("ta")
    h = lax.axis_index("ha")
    y = h // 2
    c = h - 2 * y
    h_after = lax.rem(y + 1, NY) * 2 + c
    h_before = lax.rem(y + NY - 1, NY) * 2 + c
    h_across = lax.rem(y + 2, NY) * 2 + c
    h_twin = 2 * y + 1 - c

    def remote(src, dst, send, recv, device):
        return pltpu.make_async_remote_copy(
            src_ref=src, dst_ref=dst, send_sem=send, recv_sem=recv, device_id=device, device_id_type=MESH
        )

    loads = [
        pltpu.make_async_copy(src, dst, load_sem.at[i])
        for i, (src, dst) in enumerate(((k_hbm, k_in), (v_hbm, v_in), (q_hbm, q_in)))
    ]
    for load in loads:
        load.start()

    barrier = pltpu.get_barrier_semaphore()
    partners = [{"ta": lax.rem(z + k, NT)} for k in range(1, NT)]
    partners += [{"ha": h_after}, {"ha": h_before}, {"ha": h_twin}]
    for partner in partners:
        pl.semaphore_signal(barrier, inc=1, device_id=partner, device_id_type=MESH)

    def to(k):
        return lax.rem(z + k, NT)

    def came(k):
        return lax.rem(z + NT - k, NT)

    def far_copy(k):
        return remote(far_in, far_all.at[z], far_s.at[k], far_r.at[k], {"ta": to(k)})

    def kv_copy(j, k):
        return remote(
            kv_out.at[to(k) * GROUP + j], tables[j].at[z * NH + h], z_s.at[j, k], z_r.at[j, k], {"ta": to(k)}
        )

    def q_copy(j, k):
        return remote(q_out.at[to(k) * GROUP + j], q_all.at[j, z], q_s.at[j, k], q_r.at[j, k], {"ta": to(k)})

    def o_copy(j, k):
        return remote(o_out.at[j, to(k)], o_in.at[z * GROUP + j], o_s.at[j, k], o_r.at[j, k], {"ta": to(k)})

    def y_copy(j, k, i):
        table = tables[j]
        base = came(k) * NH

        def slab(row):
            return table.at[base + row]

        if i < 3:
            src = kv_out.at[z * GROUP + j] if k == 0 else slab(h)
            dst = slab(h)
            device = (h_after, h_before, h_twin)[i]
        elif i == 3:
            src = dst = table.at[base + h_before, 0]
            device = h_after
        elif i == 4:
            src = dst = table.at[base + h_after, 1]
            device = h_before
        else:
            src = dst = slab((h_before, h_after, h_across)[i - 5])
            device = h_twin
        return remote(src, dst, y_s.at[j, k, i], y_r.at[j, k, i], {"ha": device})

    def own_kv(j):
        return pltpu.make_async_copy(kv_out.at[z * GROUP + j], tables[j].at[z * NH + h], own_sem.at[j, 0])

    def own_q(j):
        return pltpu.make_async_copy(q_out.at[z * GROUP + j], q_all.at[j, z], own_sem.at[j, 1])

    def own_o(j):
        return pltpu.make_async_copy(o_out.at[j, z], o_in.at[z * GROUP + j], own_sem.at[j, 2])

    own_far = pltpu.make_async_copy(far_in, far_all.at[z], own_sem.at[0, 3])

    def lanes(head):
        return pl.ds(pl.multiple_of(head * HD, HD), HD)

    own_far.start()
    loads[0].wait()
    loads[1].wait()
    for j in range(GROUP):
        for k in range(NT):
            head = to(k) * GROUP + j
            for i, source in enumerate((k_in, v_in)):
                for w, tile in enumerate(untile(source[:, :, :, lanes(head)])):
                    kv_out[head, i, w] = tile
        if j == 0:
            pl.semaphore_wait(barrier, len(partners))
        for k in range(1, NT):
            kv_copy(j, k).start()
        for i in range(3):
            y_copy(j, 0, i).start()
        own_kv(j).start()
    for k in range(1, NT):
        far_copy(k).start()
    loads[2].wait()
    for j in range(GROUP):
        for k in range(NT):
            head = to(k) * GROUP + j
            for w, tile in enumerate(untile(q_in[:, :, :, lanes(head)])):
                q_out[head, w] = tile
        own_q(j).start()

    def send_queries():
        for j in range(GROUP):
            for k in range(1, NT):
                q_copy(j, k).start()

    at_end = jnp.logical_or(z == 0, z == NT - 1)
    pl.when(jnp.logical_not(at_end))(send_queries)

    def step_d(j, k):
        y_copy(j, k, 0).wait_recv()
        y_copy(j, k, 3).start()
        y_copy(j, k, 5).start()
        y_copy(j, k, 1).wait_recv()
        y_copy(j, k, 4).start()
        y_copy(j, k, 6).start()

    def step_e(j, k):
        y_copy(j, k, 3).wait_recv()
        y_copy(j, k, 4).wait_recv()
        y_copy(j, k, 7).start()

    def unit(j, t, w):
        table = tables[j]
        q = q_all[j, t, w]
        near = (
            (t, h, None),
            (jnp.maximum(t - 1, 0), h, t > 0),
            (jnp.minimum(t + 1, NT - 1), h, t < NT - 1),
            (t, jnp.maximum(h - 1, 0), h > 0),
            (t, jnp.minimum(h + 1, NH - 1), h < NH - 1),
        )
        ids = [far_all[t, w, f, z * GROUP + j] for f in range(FAR)]
        contract = (((1,), (1,)), ((), ()))
        high = None

        def score(keys, start, bias, high):
            s = lax.dot_general(q, keys, contract, preferred_element_type=jnp.float32)
            if bias is not None:
                s = s + bias
            scores[w, :, start : start + keys.shape[0]] = s
            for at in range(0, keys.shape[0], HD):
                part = s[:, at : at + HD]
                high = part if high is None else jnp.maximum(high, part)
            return high

        for n, (tt, hh, there) in enumerate(near):
            keys = table[tt * NH + hh, 0].reshape(SLAB, HD)
            bias = None if there is None else jnp.where(there, 0.0, MASKED).astype(jnp.float32)
            high = score(keys, n * SLAB, bias, high)
        for f, tile in enumerate(ids):
            high = score(table[tile // 2, 0, lax.rem(tile, 2)], 5 * SLAB + f * TILE, None, high)
        top = jnp.max(high, axis=1, keepdims=True)
        accum = jnp.zeros((TILE, 2 * HD), jnp.float32)

        def gather(values, start, accum):
            s = scores[w, :, start : start + values.shape[0]]
            p = jnp.exp2((s - top) * EXP2_SCALE).astype(jnp.bfloat16)
            wide = jnp.concatenate((values, jnp.ones_like(values)), axis=1)
            return accum + jnp.dot(p, wide, preferred_element_type=jnp.float32)

        for n, (tt, hh, _) in enumerate(near):
            accum = gather(table[tt * NH + hh, 1].reshape(SLAB, HD), n * SLAB, accum)
        for f, tile in enumerate(ids):
            accum = gather(table[tile // 2, 1, lax.rem(tile, 2)], 5 * SLAB + f * TILE, accum)
        o_out[j, t, w] = (accum[:, :HD] / accum[:, HD:]).astype(jnp.bfloat16)

    def attend(j):
        if j == 0:
            own_far.wait()
            for k in range(1, NT):
                far_copy(k).wait_recv()
        own_kv(j).wait()
        own_q(j).wait()
        for k in range(1, NT):
            q_copy(j, k).wait_recv()
        for k in range(NT):
            for i in (2, 5, 6, 7):
                y_copy(j, k, i).wait_recv()

        def queries_of(k, carry):
            t = to(k)
            for w in range(2):
                unit(j, t, w)

            @pl.when(k < NT)
            def _():
                o_copy(j, k).start()

            return carry

        lax.fori_loop(1, NT + 1, queries_of, 0)
        own_o(j).start()

    def write(j, k):
        head = came(k) * GROUP + j
        return pltpu.make_async_copy(out.at[:, :, :, lanes(head)], out_hbm.at[:, :, :, lanes(head)], out_sem.at[j, k])

    def collect(j):
        own_o(j).wait()
        for k in range(NT):
            if k:
                o_copy(j, k).wait_recv()
            head = came(k) * GROUP + j
            x = [o_in[head, w].astype(jnp.float32).reshape(32, 8, HD) for w in range(2)]
            out[:, :, :, lanes(head)] = (
                jnp.concatenate(x, axis=1).astype(jnp.bfloat16).reshape(4, 8, 16, HD)
            )
            write(j, k).start()

    for step, j, k in STEPS:
        if step == "C":
            kv_copy(j, k).wait_recv()
            for i in range(3):
                y_copy(j, k, i).start()
        elif step == "D":
            step_d(j, k)
        elif step == "E":
            step_e(j, k)
        elif step == "Q":
            pl.when(at_end)(send_queries)
        elif step == "X":
            attend(j)
        else:
            collect(j)

    for k in range(1, NT):
        far_copy(k).wait_send()
    for j in range(GROUP):
        for k in range(NT):
            if k:
                kv_copy(j, k).wait_send()
                q_copy(j, k).wait_send()
                o_copy(j, k).wait_send()
            for i in range(8):
                y_copy(j, k, i).wait_send()
            write(j, k).wait()


def body(queries, keys, values, far_tiles):
    bf = jnp.bfloat16
    far_tiles = jnp.transpose(far_tiles, (0, 2, 1))
    any_space = pl.BlockSpec(memory_space=pl.ANY)
    dma = pltpu.SemaphoreType.DMA
    table = pltpu.VMEM((NT * NH, 2, 2, TILE, HD), bf)
    slab = pltpu.VMEM(queries.shape, bf)
    return pl.pallas_call(
        kernel,
        out_shape=jax.ShapeDtypeStruct(queries.shape, bf),
        in_specs=[any_space] * 3 + [pl.BlockSpec(memory_space=pltpu.SMEM)],
        out_specs=any_space,
        scratch_shapes=[
            slab, slab, slab, slab,
            pltpu.VMEM((HEADS, 2, 2, TILE, HD), bf),
            pltpu.VMEM((HEADS, 2, TILE, HD), bf),
            table, table, table,
            pltpu.VMEM((GROUP, NT, 2, TILE, HD), bf),
            pltpu.VMEM((GROUP, NT, 2, TILE, HD), bf),
            pltpu.VMEM((HEADS, 2, TILE, HD), bf),
            pltpu.SMEM((NT,) + far_tiles.shape, jnp.int32),
            pltpu.VMEM((2, TILE, KEYS), jnp.float32),
            dma((3,)), dma((GROUP, 4)), dma((GROUP, NT)), dma((NT,)), dma((NT,)),
            dma((GROUP, NT)), dma((GROUP, NT)), dma((GROUP, NT)), dma((GROUP, NT)), dma((GROUP, NT)), dma((GROUP, NT)),
            dma((GROUP, NT, 8)), dma((GROUP, NT, 8)),
        ],
        compiler_params=pltpu.CompilerParams(
            collective_id=0, has_side_effects=True, vmem_limit_bytes=60 << 20
        ),
    )(queries, keys, values, far_tiles)


def solution(mesh):
    spec = P(("vid", "ta"), "ha", None, None)
    in_specs = (spec, spec, spec, P(("vid", "ta", "ha"), None, None))
    return jax.shard_map(body, mesh=mesh, in_specs=in_specs, out_specs=spec, check_vma=False)
```

```python
import functools

import jax
import jax.numpy as jnp
from jax import lax
from jax.experimental import pallas as pl
from jax.experimental.pallas import tpu as pltpu
from jax.sharding import PartitionSpec as P

HEADS = 12
HD = 128
FAR = 4
NT = 4
NH = 8
NY = 4
GROUP = HEADS // NT
TILE = 256
SLAB = 512
KEYS = 5 * SLAB + FAR * TILE
EXP2_SCALE = HD**-0.5 * 1.4426950408889634
MASKED = -1e30
MESH = pl.DeviceIdType.MESH

STEPS = (
    ("C", 0, 1), ("D", 0, 0), ("C", 0, 2), ("D", 1, 0), ("C", 2, 0), ("E", 0, 0), ("D", 0, 1), ("E", 1, 0),
    ("D", 0, 2), ("E", 0, 1), ("C", 1, 1), ("C", 0, 3), ("C", 1, 2), ("D", 2, 0), ("E", 0, 2), ("D", 1, 1),
    ("E", 2, 0), ("C", 2, 1), ("D", 0, 3), ("E", 1, 1), ("D", 1, 2), ("C", 1, 3), ("C", 2, 2), ("E", 0, 3),
    ("E", 1, 2), ("D", 2, 1), ("X", 0, 0), ("E", 2, 1), ("C", 2, 3), ("Q", 0, 0), ("D", 1, 3), ("X", 0, 1),
    ("D", 2, 2), ("E", 1, 3), ("E", 2, 2), ("X", 1, 0), ("D", 2, 3), ("X", 1, 1), ("E", 2, 3), ("X", 2, 0),
    ("X", 2, 1), ("W", 0, 0), ("W", 1, 0), ("W", 2, 0),
)


def untile(block):
    x = block.astype(jnp.float32).reshape(32, 2, 8, HD)
    return [x[:, w].reshape(TILE, HD).astype(jnp.bfloat16) for w in range(2)]


def kernel(
    q_hbm, k_hbm, v_hbm, far_in, out_hbm,
    out, q_in, k_in, v_in, kv_out, q_out, t0, t1, t2, q_all, o_out, o_in, far_all, scores,
    load_sem, own_sem, out_sem, far_s, far_r, z_s, z_r, q_s, q_r, o_s, o_r, y_s, y_r,
):
    tables = (t0, t1, t2)
    z = lax.axis_index("ta")
    h = lax.axis_index("ha")
    y = h // 2
    c = h - 2 * y
    h_after = lax.rem(y + 1, NY) * 2 + c
    h_before = lax.rem(y + NY - 1, NY) * 2 + c
    h_across = lax.rem(y + 2, NY) * 2 + c
    h_twin = 2 * y + 1 - c

    def remote(src, dst, send, recv, device):
        return pltpu.make_async_remote_copy(
            src_ref=src, dst_ref=dst, send_sem=send, recv_sem=recv, device_id=device, device_id_type=MESH
        )

    loads = [
        pltpu.make_async_copy(src, dst, load_sem.at[i])
        for i, (src, dst) in enumerate(((k_hbm, k_in), (v_hbm, v_in), (q_hbm, q_in)))
    ]
    for load in loads:
        load.start()

    barrier = pltpu.get_barrier_semaphore()
    partners = [{"ta": lax.rem(z + k, NT)} for k in range(1, NT)]
    partners += [{"ha": h_after}, {"ha": h_before}, {"ha": h_twin}]
    for partner in partners:
        pl.semaphore_signal(barrier, inc=1, device_id=partner, device_id_type=MESH)

    def to(k):
        return lax.rem(z + k, NT)

    def came(k):
        return lax.rem(z + NT - k, NT)

    first = 1 + (z // 2) * (1 - lax.rem(z, 2))
    second = 3 - lax.rem(z, 2) * (1 - z // 2)
    order = (0, first, second, 6 - first - second)

    def far_copy(k):
        return remote(far_in, far_all.at[z], far_s.at[k], far_r.at[k], {"ta": to(k)})

    def kv_copy(j, k):
        return remote(
            kv_out.at[to(k) * GROUP + j], tables[j].at[z * NH + h], z_s.at[j, k], z_r.at[j, k], {"ta": to(k)}
        )

    def q_copy(j, k):
        return remote(q_out.at[to(k) * GROUP + j], q_all.at[j, z], q_s.at[j, k], q_r.at[j, k], {"ta": to(k)})

    def o_copy(j, k):
        return remote(o_out.at[j, to(k)], o_in.at[z * GROUP + j], o_s.at[j, k], o_r.at[j, k], {"ta": to(k)})

    def y_copy(j, r, i):
        table = tables[j]
        base = came(order[r]) * NH

        def slab(row):
            return table.at[base + row]

        if i < 3:
            src = kv_out.at[z * GROUP + j] if r == 0 else slab(h)
            dst = slab(h)
            device = (h_after, h_before, h_twin)[i]
        elif i == 3:
            src = dst = table.at[base + h_before, 0]
            device = h_after
        elif i == 4:
            src = dst = table.at[base + h_after, 1]
            device = h_before
        else:
            src = dst = slab((h_before, h_after, h_across)[i - 5])
            device = h_twin
        return remote(src, dst, y_s.at[j, r, i], y_r.at[j, r, i], {"ha": device})

    def own_kv(j):
        return pltpu.make_async_copy(kv_out.at[z * GROUP + j], tables[j].at[z * NH + h], own_sem.at[j, 0])

    def own_q(j):
        return pltpu.make_async_copy(q_out.at[z * GROUP + j], q_all.at[j, z], own_sem.at[j, 1])

    def own_o(j):
        return pltpu.make_async_copy(o_out.at[j, z], o_in.at[z * GROUP + j], own_sem.at[j, 2])

    own_far = pltpu.make_async_copy(far_in, far_all.at[z], own_sem.at[0, 3])

    def lanes(head):
        return pl.ds(pl.multiple_of(head * HD, HD), HD)

    def pass_on(j, r):
        for i in range(3):
            y_copy(j, r, i).start()

    own_far.start()
    def prepare_queries(j):
        for k in range(NT):
            head = to(k) * GROUP + j
            for w, tile in enumerate(untile(q_in[:, :, :, lanes(head)])):
                q_out[head, w] = tile
        own_q(j).start()

    def send_queries(j):
        for k in range(1, NT):
            q_copy(j, k).start()

    loads[0].wait()
    loads[1].wait()
    for j in range(GROUP):
        for k in range(NT):
            head = to(k) * GROUP + j
            for i, source in enumerate((k_in, v_in)):
                for w, tile in enumerate(untile(source[:, :, :, lanes(head)])):
                    kv_out[head, i, w] = tile
        if j == 0:
            pl.semaphore_wait(barrier, len(partners))
        for k in range(1, NT):
            kv_copy(j, k).start()
        if j < GROUP - 1:
            pass_on(j, 0)
        own_kv(j).start()
        if j == 1:
            loads[2].wait()
            prepare_queries(0)
            send_queries(0)
    for k in range(1, NT):
        far_copy(k).start()
    for j in range(1, GROUP):
        prepare_queries(j)

    at_end = jnp.logical_or(z == 0, z == NT - 1)

    def send_rest():
        for j in range(1, GROUP):
            send_queries(j)

    pl.when(jnp.logical_not(at_end))(send_rest)

    def step_d(j, r):
        y_copy(j, r, 0).wait_recv()
        y_copy(j, r, 3).start()
        y_copy(j, r, 5).start()
        y_copy(j, r, 1).wait_recv()
        y_copy(j, r, 4).start()
        y_copy(j, r, 6).start()

    def step_e(j, r):
        y_copy(j, r, 3).wait_recv()
        y_copy(j, r, 4).wait_recv()
        y_copy(j, r, 7).start()

    def unit(j, t, w):
        table = tables[j]
        q = q_all[j, t, w]
        near = (
            (t, h, None),
            (jnp.maximum(t - 1, 0), h, t > 0),
            (jnp.minimum(t + 1, NT - 1), h, t < NT - 1),
            (t, jnp.maximum(h - 1, 0), h > 0),
            (t, jnp.minimum(h + 1, NH - 1), h < NH - 1),
        )
        ids = [far_all[t, w, f, z * GROUP + j] for f in range(FAR)]
        contract = (((1,), (1,)), ((), ()))
        high = None

        def score(keys, start, bias, high):
            s = lax.dot_general(q, keys, contract, preferred_element_type=jnp.float32)
            if bias is not None:
                s = s + bias
            scores[w, :, start : start + keys.shape[0]] = s
            for at in range(0, keys.shape[0], HD):
                part = s[:, at : at + HD]
                high = part if high is None else jnp.maximum(high, part)
            return high

        for n, (tt, hh, there) in enumerate(near):
            keys = table[tt * NH + hh, 0].reshape(SLAB, HD)
            bias = None if there is None else jnp.where(there, 0.0, MASKED).astype(jnp.float32)
            high = score(keys, n * SLAB, bias, high)
        for f, tile in enumerate(ids):
            high = score(table[tile // 2, 0, lax.rem(tile, 2)], 5 * SLAB + f * TILE, None, high)
        top = jnp.max(high, axis=1, keepdims=True)
        accum = jnp.zeros((TILE, 2 * HD), jnp.float32)

        def gather(values, start, accum):
            s = scores[w, :, start : start + values.shape[0]]
            p = jnp.exp2((s - top) * EXP2_SCALE).astype(jnp.bfloat16)
            wide = jnp.concatenate((values, jnp.ones_like(values)), axis=1)
            return accum + jnp.dot(p, wide, preferred_element_type=jnp.float32)

        for n, (tt, hh, _) in enumerate(near):
            accum = gather(table[tt * NH + hh, 1].reshape(SLAB, HD), n * SLAB, accum)
        for f, tile in enumerate(ids):
            accum = gather(table[tile // 2, 1, lax.rem(tile, 2)], 5 * SLAB + f * TILE, accum)
        o_out[j, t, w] = (accum[:, :HD] / accum[:, HD:]).astype(jnp.bfloat16)

    def attend(j, half):
        if half == 0:
            if j == 0:
                own_far.wait()
                for k in range(1, NT):
                    far_copy(k).wait_recv()
            own_kv(j).wait()
            own_q(j).wait()
            for k in range(1, NT):
                q_copy(j, k).wait_recv()
            for r in range(NT):
                for i in (2, 5, 6, 7):
                    y_copy(j, r, i).wait_recv()

        def queries_of(k, carry):
            t = to(k)
            for w in range(2):
                unit(j, t, w)

            @pl.when(k < NT)
            def _():
                o_copy(j, k).start()

            return carry

        lax.fori_loop(2 * half + 1, 2 * half + 3, queries_of, 0)
        if half:
            own_o(j).start()

    def write(j, k):
        head = came(k) * GROUP + j
        return pltpu.make_async_copy(out.at[:, :, :, lanes(head)], out_hbm.at[:, :, :, lanes(head)], out_sem.at[j, k])

    def collect(j):
        own_o(j).wait()
        for k in range(NT):
            if k:
                o_copy(j, k).wait_recv()
            head = came(k) * GROUP + j
            x = [o_in[head, w].astype(jnp.float32).reshape(32, 8, HD) for w in range(2)]
            out[:, :, :, lanes(head)] = (
                jnp.concatenate(x, axis=1).astype(jnp.bfloat16).reshape(4, 8, 16, HD)
            )
            write(j, k).start()

    for step, j, r in STEPS:
        if step == "C":
            if r:
                kv_copy(j, order[r]).wait_recv()
            pass_on(j, r)
        elif step == "D":
            step_d(j, r)
        elif step == "E":
            step_e(j, r)
        elif step == "Q":
            pl.when(at_end)(send_rest)
        elif step == "X":
            attend(j, r)
        else:
            collect(j)

    for k in range(1, NT):
        far_copy(k).wait_send()
    for j in range(GROUP):
        for k in range(NT):
            if k:
                kv_copy(j, k).wait_send()
                q_copy(j, k).wait_send()
                o_copy(j, k).wait_send()
            for i in range(8):
                y_copy(j, k, i).wait_send()
            write(j, k).wait()


def body(queries, keys, values, far_tiles):
    bf = jnp.bfloat16
    far_tiles = jnp.transpose(far_tiles, (0, 2, 1))
    any_space = pl.BlockSpec(memory_space=pl.ANY)
    dma = pltpu.SemaphoreType.DMA
    table = pltpu.VMEM((NT * NH, 2, 2, TILE, HD), bf)
    slab = pltpu.VMEM(queries.shape, bf)
    return pl.pallas_call(
        kernel,
        out_shape=jax.ShapeDtypeStruct(queries.shape, bf),
        in_specs=[any_space] * 3 + [pl.BlockSpec(memory_space=pltpu.SMEM)],
        out_specs=any_space,
        scratch_shapes=[
            slab, slab, slab, slab,
            pltpu.VMEM((HEADS, 2, 2, TILE, HD), bf),
            pltpu.VMEM((HEADS, 2, TILE, HD), bf),
            table, table, table,
            pltpu.VMEM((GROUP, NT, 2, TILE, HD), bf),
            pltpu.VMEM((GROUP, NT, 2, TILE, HD), bf),
            pltpu.VMEM((HEADS, 2, TILE, HD), bf),
            pltpu.SMEM((NT,) + far_tiles.shape, jnp.int32),
            pltpu.VMEM((2, TILE, KEYS), jnp.float32),
            dma((3,)), dma((GROUP, 4)), dma((GROUP, NT)), dma((NT,)), dma((NT,)),
            dma((GROUP, NT)), dma((GROUP, NT)), dma((GROUP, NT)), dma((GROUP, NT)), dma((GROUP, NT)), dma((GROUP, NT)),
            dma((GROUP, NT, 8)), dma((GROUP, NT, 8)),
        ],
        compiler_params=pltpu.CompilerParams(
            collective_id=0, has_side_effects=True, vmem_limit_bytes=60 << 20
        ),
    )(queries, keys, values, far_tiles)


def solution(mesh):
    spec = P(("vid", "ta"), "ha", None, None)
    in_specs = (spec, spec, spec, P(("vid", "ta", "ha"), None, None))
    return jax.shard_map(body, mesh=mesh, in_specs=in_specs, out_specs=spec, check_vma=False)
```

```python
import functools

import jax
import jax.numpy as jnp
from jax import lax
from jax.experimental import pallas as pl
from jax.experimental.pallas import tpu as pltpu
from jax.sharding import PartitionSpec as P

HEADS = 12
HD = 128
FAR = 4
NT = 4
NH = 8
NY = 4
GROUP = HEADS // NT
TILE = 256
SLAB = 512
KEYS = 5 * SLAB + FAR * TILE
EXP2_SCALE = HD**-0.5 * 1.4426950408889634
MASKED = -1e30
MESH = pl.DeviceIdType.MESH

STEPS = (
    ("C", 0, 1), ("D", 0, 0), ("C", 0, 2), ("D", 1, 0), ("C", 2, 0), ("E", 0, 0), ("D", 0, 1), ("E", 1, 0),
    ("D", 0, 2), ("E", 0, 1), ("C", 1, 1), ("C", 0, 3), ("C", 1, 2), ("D", 2, 0), ("E", 0, 2), ("D", 1, 1),
    ("E", 2, 0), ("C", 2, 1), ("D", 0, 3), ("E", 1, 1), ("D", 1, 2), ("C", 1, 3), ("C", 2, 2), ("E", 0, 3),
    ("E", 1, 2), ("D", 2, 1), ("X", 0, 0), ("E", 2, 1), ("C", 2, 3), ("D", 1, 3), ("Q", 0, 0), ("X", 0, 1),
    ("D", 2, 2), ("E", 1, 3), ("E", 2, 2), ("X", 1, 0), ("D", 2, 3), ("X", 1, 1), ("E", 2, 3), ("X", 2, 0),
    ("X", 2, 1), ("W", 0, 0), ("W", 1, 0), ("W", 2, 0),
)


def untile(block):
    x = block.astype(jnp.float32).reshape(32, 2, 8, HD)
    return [x[:, w].reshape(TILE, HD).astype(jnp.bfloat16) for w in range(2)]


def kernel(
    q_hbm, k_hbm, v_hbm, far_in, out_hbm,
    out, q_in, k_in, v_in, kv_out, q_out, t0, t1, t2, q_all, o_out, o_in, far_all, scores,
    load_sem, own_sem, out_sem, far_s, far_r, z_s, z_r, q_s, q_r, o_s, o_r, y_s, y_r,
):
    tables = (t0, t1, t2)
    z = lax.axis_index("ta")
    h = lax.axis_index("ha")
    y = h // 2
    c = h - 2 * y
    h_after = lax.rem(y + 1, NY) * 2 + c
    h_before = lax.rem(y + NY - 1, NY) * 2 + c
    h_across = lax.rem(y + 2, NY) * 2 + c
    h_twin = 2 * y + 1 - c

    def remote(src, dst, send, recv, device):
        return pltpu.make_async_remote_copy(
            src_ref=src, dst_ref=dst, send_sem=send, recv_sem=recv, device_id=device, device_id_type=MESH
        )

    loads = [
        pltpu.make_async_copy(src, dst, load_sem.at[i])
        for i, (src, dst) in enumerate(((k_hbm, k_in), (v_hbm, v_in), (q_hbm, q_in)))
    ]
    for load in loads:
        load.start()

    barrier = pltpu.get_barrier_semaphore()
    partners = [{"ta": lax.rem(z + k, NT)} for k in range(1, NT)]
    partners += [{"ha": h_after}, {"ha": h_before}, {"ha": h_twin}]
    for partner in partners:
        pl.semaphore_signal(barrier, inc=1, device_id=partner, device_id_type=MESH)

    def to(k):
        return lax.rem(z + k, NT)

    def came(k):
        return lax.rem(z + NT - k, NT)

    first = 1 + (z // 2) * (1 - lax.rem(z, 2))
    second = 3 - lax.rem(z, 2) * (1 - z // 2)
    order = (0, first, second, 6 - first - second)

    def far_copy(k):
        return remote(far_in, far_all.at[z], far_s.at[k], far_r.at[k], {"ta": to(k)})

    def kv_copy(j, k):
        return remote(
            kv_out.at[to(k) * GROUP + j], tables[j].at[z * NH + h], z_s.at[j, k], z_r.at[j, k], {"ta": to(k)}
        )

    def q_copy(j, k):
        return remote(q_out.at[to(k) * GROUP + j], q_all.at[j, z], q_s.at[j, k], q_r.at[j, k], {"ta": to(k)})

    def o_copy(j, k):
        return remote(o_out.at[j, to(k)], o_in.at[z * GROUP + j], o_s.at[j, k], o_r.at[j, k], {"ta": to(k)})

    def y_copy(j, r, i):
        table = tables[j]
        base = came(order[r]) * NH

        def slab(row):
            return table.at[base + row]

        if i < 3:
            src = kv_out.at[z * GROUP + j] if r == 0 else slab(h)
            dst = slab(h)
            device = (h_after, h_before, h_twin)[i]
        elif i == 3:
            src = dst = table.at[base + h_before, 0]
            device = h_after
        elif i == 4:
            src = dst = table.at[base + h_after, 1]
            device = h_before
        else:
            src = dst = slab((h_before, h_after, h_across)[i - 5])
            device = h_twin
        return remote(src, dst, y_s.at[j, r, i], y_r.at[j, r, i], {"ha": device})

    def own_kv(j):
        return pltpu.make_async_copy(kv_out.at[z * GROUP + j], tables[j].at[z * NH + h], own_sem.at[j, 0])

    def own_q(j):
        return pltpu.make_async_copy(q_out.at[z * GROUP + j], q_all.at[j, z], own_sem.at[j, 1])

    def own_o(j):
        return pltpu.make_async_copy(o_out.at[j, z], o_in.at[z * GROUP + j], own_sem.at[j, 2])

    own_far = pltpu.make_async_copy(far_in, far_all.at[z], own_sem.at[0, 3])

    def lanes(head):
        return pl.ds(pl.multiple_of(head * HD, HD), HD)

    def pass_on(j, r):
        for i in range(3):
            y_copy(j, r, i).start()

    own_far.start()
    def prepare_queries(j):
        for k in range(NT):
            head = to(k) * GROUP + j
            for w, tile in enumerate(untile(q_in[:, :, :, lanes(head)])):
                q_out[head, w] = tile
        own_q(j).start()

    def send_queries(j):
        for k in range(1, NT):
            q_copy(j, k).start()

    loads[0].wait()
    loads[1].wait()
    for j in range(GROUP):
        for k in range(NT):
            head = to(k) * GROUP + j
            for i, source in enumerate((k_in, v_in)):
                for w, tile in enumerate(untile(source[:, :, :, lanes(head)])):
                    kv_out[head, i, w] = tile
        if j == 0:
            pl.semaphore_wait(barrier, len(partners))
        for k in range(1, NT):
            kv_copy(j, k).start()
        if j < GROUP - 1:
            pass_on(j, 0)
        own_kv(j).start()
        if j == 1:
            loads[2].wait()
            prepare_queries(0)
            send_queries(0)
    for k in range(1, NT):
        far_copy(k).start()
    for j in range(1, GROUP):
        prepare_queries(j)

    at_end = jnp.logical_or(z == 0, z == NT - 1)

    def send_rest():
        for j in range(1, GROUP):
            send_queries(j)

    pl.when(jnp.logical_not(at_end))(send_rest)

    def step_d(j, r):
        y_copy(j, r, 0).wait_recv()
        y_copy(j, r, 3).start()
        y_copy(j, r, 5).start()
        y_copy(j, r, 1).wait_recv()
        y_copy(j, r, 4).start()
        y_copy(j, r, 6).start()

    def step_e(j, r):
        y_copy(j, r, 3).wait_recv()
        y_copy(j, r, 4).wait_recv()
        y_copy(j, r, 7).start()

    def unit(j, t, w):
        table = tables[j]
        q = q_all[j, t, w]
        near = (
            (t, h, None),
            (jnp.maximum(t - 1, 0), h, t > 0),
            (jnp.minimum(t + 1, NT - 1), h, t < NT - 1),
            (t, jnp.maximum(h - 1, 0), h > 0),
            (t, jnp.minimum(h + 1, NH - 1), h < NH - 1),
        )
        ids = [far_all[t, w, f, z * GROUP + j] for f in range(FAR)]
        contract = (((1,), (1,)), ((), ()))
        high = None

        def score(keys, start, bias, high):
            s = lax.dot_general(q, keys, contract, preferred_element_type=jnp.float32)
            if bias is not None:
                s = s + bias
            scores[w, :, start : start + keys.shape[0]] = s
            for at in range(0, keys.shape[0], HD):
                part = s[:, at : at + HD]
                high = part if high is None else jnp.maximum(high, part)
            return high

        for n, (tt, hh, there) in enumerate(near):
            keys = table[tt * NH + hh, 0].reshape(SLAB, HD)
            bias = None if there is None else jnp.where(there, 0.0, MASKED).astype(jnp.float32)
            high = score(keys, n * SLAB, bias, high)
        for f, tile in enumerate(ids):
            high = score(table[tile // 2, 0, lax.rem(tile, 2)], 5 * SLAB + f * TILE, None, high)
        top = jnp.max(high, axis=1, keepdims=True)
        accum = jnp.zeros((TILE, 2 * HD), jnp.float32)

        def gather(values, start, accum):
            s = scores[w, :, start : start + values.shape[0]]
            p = jnp.exp2((s - top) * EXP2_SCALE).astype(jnp.bfloat16)
            wide = jnp.concatenate((values, jnp.ones_like(values)), axis=1)
            return accum + jnp.dot(p, wide, preferred_element_type=jnp.float32)

        for n, (tt, hh, _) in enumerate(near):
            accum = gather(table[tt * NH + hh, 1].reshape(SLAB, HD), n * SLAB, accum)
        for f, tile in enumerate(ids):
            accum = gather(table[tile // 2, 1, lax.rem(tile, 2)], 5 * SLAB + f * TILE, accum)
        o_out[j, t, w] = (accum[:, :HD] / accum[:, HD:]).astype(jnp.bfloat16)

    def attend(j, half):
        if half == 0:
            if j == 0:
                own_far.wait()
                for k in range(1, NT):
                    far_copy(k).wait_recv()
            own_kv(j).wait()
            own_q(j).wait()
            for k in range(1, NT):
                q_copy(j, k).wait_recv()
            for r in range(NT):
                for i in (2, 5, 6, 7):
                    y_copy(j, r, i).wait_recv()

        def queries_of(k, carry):
            t = to(k)
            for w in range(2):
                unit(j, t, w)

            @pl.when(k < NT)
            def _():
                o_copy(j, k).start()

            return carry

        lax.fori_loop(2 * half + 1, 2 * half + 3, queries_of, 0)
        if half:
            own_o(j).start()

    def write(j, k):
        head = came(k) * GROUP + j
        return pltpu.make_async_copy(out.at[:, :, :, lanes(head)], out_hbm.at[:, :, :, lanes(head)], out_sem.at[j, k])

    def collect(j):
        own_o(j).wait()
        for k in range(NT):
            if k:
                o_copy(j, k).wait_recv()
            head = came(k) * GROUP + j
            x = [o_in[head, w].astype(jnp.float32).reshape(32, 8, HD) for w in range(2)]
            out[:, :, :, lanes(head)] = (
                jnp.concatenate(x, axis=1).astype(jnp.bfloat16).reshape(4, 8, 16, HD)
            )
            write(j, k).start()

    for step, j, r in STEPS:
        if step == "C":
            if r:
                kv_copy(j, order[r]).wait_recv()
            pass_on(j, r)
        elif step == "D":
            step_d(j, r)
        elif step == "E":
            step_e(j, r)
        elif step == "Q":
            pl.when(at_end)(send_rest)
        elif step == "X":
            attend(j, r)
        else:
            collect(j)

    for k in range(1, NT):
        far_copy(k).wait_send()
    for j in range(GROUP):
        for k in range(NT):
            if k:
                kv_copy(j, k).wait_send()
                q_copy(j, k).wait_send()
                o_copy(j, k).wait_send()
            for i in range(8):
                y_copy(j, k, i).wait_send()
            write(j, k).wait()


def body(queries, keys, values, far_tiles):
    bf = jnp.bfloat16
    far_tiles = jnp.transpose(far_tiles, (0, 2, 1))
    any_space = pl.BlockSpec(memory_space=pl.ANY)
    dma = pltpu.SemaphoreType.DMA
    table = pltpu.VMEM((NT * NH, 2, 2, TILE, HD), bf)
    slab = pltpu.VMEM(queries.shape, bf)
    return pl.pallas_call(
        kernel,
        out_shape=jax.ShapeDtypeStruct(queries.shape, bf),
        in_specs=[any_space] * 3 + [pl.BlockSpec(memory_space=pltpu.SMEM)],
        out_specs=any_space,
        scratch_shapes=[
            slab, slab, slab, slab,
            pltpu.VMEM((HEADS, 2, 2, TILE, HD), bf),
            pltpu.VMEM((HEADS, 2, TILE, HD), bf),
            table, table, table,
            pltpu.VMEM((GROUP, NT, 2, TILE, HD), bf),
            pltpu.VMEM((GROUP, NT, 2, TILE, HD), bf),
            pltpu.VMEM((HEADS, 2, TILE, HD), bf),
            pltpu.SMEM((NT,) + far_tiles.shape, jnp.int32),
            pltpu.VMEM((2, TILE, KEYS), jnp.float32),
            dma((3,)), dma((GROUP, 4)), dma((GROUP, NT)), dma((NT,)), dma((NT,)),
            dma((GROUP, NT)), dma((GROUP, NT)), dma((GROUP, NT)), dma((GROUP, NT)), dma((GROUP, NT)), dma((GROUP, NT)),
            dma((GROUP, NT, 8)), dma((GROUP, NT, 8)),
        ],
        compiler_params=pltpu.CompilerParams(
            collective_id=0, has_side_effects=True, vmem_limit_bytes=60 << 20
        ),
    )(queries, keys, values, far_tiles)


def solution(mesh):
    spec = P(("vid", "ta"), "ha", None, None)
    in_specs = (spec, spec, spec, P(("vid", "ta", "ha"), None, None))
    return jax.shard_map(body, mesh=mesh, in_specs=in_specs, out_specs=spec, check_vma=False)
```
